256 devices in a mesh: ctx: 32 (over y, z_lo, core), tp: 8 (over z_hi, x).
Axes of the slice: x: 4, y: 4, z: 8 (z_hi: 2, z_lo: 4; z = z_hi * 4 + z_lo), core: 2. Of those that a mesh axis runs over, the one named last changes fastest.
Arguments:
- attended: bfloat16 [32768, 4096], P('ctx', 'tp'), may hold values from -6 to 6
- out_proj: bfloat16 [4096, 4096], P('tp'), may hold values from -0.09375 to 0.09375
- residual: bfloat16 [32768, 4096], P(('ctx', 'tp')), may hold values from -6 to 6
- norm_gain: float32 [4096], replicated, may hold values from 0.5 to 1.5
- cond_proj: bfloat16 [4096, 2048], P(None, 'tp'), may hold values from -0.09375 to 0.09375
- noise_proj: bfloat16 [128, 2048], P(None, 'tp'), may hold values from -0.5 to 0.5
- latent_proj: bfloat16 [2048, 128], P('tp'), may hold values from -0.176776695 to 0.176776695
- noise_draws: bfloat16 [32768, 8, 128], P('ctx'), may hold values from -6 to 6
- targets: bfloat16 [32768, 128], P(('ctx', 'tp')), may hold values from -9 to 9
Outputs:
- energies: float32 [32768], P(('ctx', 'tp'))
- cond_grad: bfloat16 [4096, 2048], P(None, 'tp')
- noise_grad: bfloat16 [128, 2048], P(None, 'tp')
- latent_grad: bfloat16 [2048, 128], P('tp')
The draws below stay inside these ranges and needn't reach their ends.
All inputs are finite; a program needn't handle non-finite values.
Results may differ from the reference program's by a relative error of at most 0.018.
Values may be sent and summed in bfloat16 or wider, within the bound.
No kernel may reach another device: no remote copies, remote signals or barrier semaphores. Data moves between devices by JAX's collectives and lax.ppermute only.
A program may use at most 128 MiB of HBM per device.

```python
import math
import jax
import jax.numpy as jnp
from jax import lax

D = 4096
HW = 2048
LAT = 128
NZ = 128
S = 8
POS = 32768
N_TP = 8


def draw_latent_proj(key, part):
    key = jax.random.fold_in(key, 11)
    position = jnp.arange(HW, dtype=jnp.float32)[:, None] / HW
    values = jax.random.truncated_normal(key, -4.0, 4.0, (HW, LAT), jnp.float32)
    scales = 0.5 * jnp.exp(position * 1.3862944)
    return (values * scales / HW ** 0.5).astype(jnp.bfloat16)


def levels(key, dims, cuts, least, high):
    gain, own = 1.0, jax.random.fold_in(key, 6)
    for axis_at, blocks in cuts:
        heights = jnp.exp(jax.random.uniform(jax.random.fold_in(own, axis_at), (blocks,), jnp.float32, least / len(cuts), high / len(cuts)))
        gain = gain * jnp.repeat(heights, dims[axis_at] // blocks).reshape([-1 if axis == axis_at else 1 for axis in range(len(dims))])
    return gain


def centred(stream_key, dims, width, bound, cuts=(), held_as=jnp.bfloat16):
    array = width * jax.random.normal(stream_key, dims, jnp.float32)
    if cuts:
        array = array * levels(stream_key, dims, cuts, -0.22, 0.18)
    return jnp.clip(array, -bound, bound).astype(held_as)


def setup_inputs(seed: int = 0) -> dict:
    keys = jax.random.split(jax.random.key(seed), 10)
    return {
        "attended": centred(keys[0], (POS, D), 1.0, 6.0, ((0, 32), (1, 8))),
        "out_proj": centred(keys[1], (D, D), D ** -0.5, 0.09375, ((0, 8),)),
        "residual": centred(keys[2], (POS, D), 1.0, 6.0, ((0, 256),)),
        "norm_gain": jnp.clip(1.0 + 0.1 * jax.random.normal(keys[3], (D,), jnp.float32), 0.5, 1.5),
        "cond_proj": centred(keys[4], (D, HW), D ** -0.5, 0.09375, ((1, 8),)),
        "noise_proj": centred(keys[5], (NZ, HW), NZ ** -0.5, 0.5, ((1, 8),)),
        "latent_proj": draw_latent_proj(jax.random.fold_in(keys[9], 71), 0),
        "noise_draws": centred(keys[7], (POS, S, NZ), 1.0, 6.0, ((0, 32),)),
        "targets": centred(keys[8], (POS, LAT), 1.5, 9.0, ((0, 256),)),
    }


def silu_slope(values):
    sigmoid = jax.nn.sigmoid(values)
    return sigmoid * (1.0 + values * (1.0 - sigmoid))

def energy_score(samples, goal_rows):
    n_draws = samples.shape[1]
    diff_t = samples - goal_rows[:, None, :]
    dist_t = jnp.sqrt(lax.optimization_barrier(jnp.sum(diff_t * diff_t, axis=-1)) + 1.0)
    diff_p = samples[:, :, None, :] - samples[:, None, :, :]
    dist_p = jnp.sqrt(lax.optimization_barrier(jnp.sum(diff_p * diff_p, axis=-1)) + 1.0)
    off_diag = 1.0 - jnp.eye(n_draws, dtype=jnp.float32)
    pair_count = n_draws * (n_draws - 1)
    energies = lax.optimization_barrier(jnp.mean(dist_t, axis=1)) - lax.optimization_barrier(jnp.sum(dist_p * off_diag, axis=(1, 2))) / (2.0 * pair_count)
    slopes = diff_t / (n_draws * dist_t[..., None]) - lax.optimization_barrier(jnp.sum(diff_p / dist_p[..., None], axis=2)) / pair_count
    return (energies, slopes.astype(jnp.bfloat16))

def widen(values):
    return lax.optimization_barrier(values).astype(jnp.float32)

def reference(attended, out_proj, residual, norm_gain, cond_proj, noise_proj, latent_proj, noise_draws, targets):
    group_width = D // N_TP
    summed = jnp.zeros((POS, D), jnp.float32)
    for group in range(N_TP):
        lower = group * group_width
        upper = lower + group_width
        partial_value = jnp.dot(attended[:, lower:upper], out_proj[lower:upper], preferred_element_type=jnp.float32).astype(jnp.bfloat16)
        summed = summed + widen(partial_value)
    hidden = residual.astype(jnp.float32) + summed
    normed = (hidden * lax.rsqrt(lax.optimization_barrier(jnp.mean(hidden * hidden, axis=-1, keepdims=True)) + 1e-05) * norm_gain).astype(jnp.bfloat16)
    block_rows = math.gcd(POS, 1024)
    blocks = POS // block_rows
    inputs = (normed.reshape(blocks, block_rows, D), noise_draws.reshape(blocks, block_rows, S, NZ), targets.reshape(blocks, block_rows, LAT))
    cond_w = cond_proj
    noise_w = noise_proj.astype(jnp.float32)
    latent_w = latent_proj.astype(jnp.float32)

    def head_block(grads, pieces):
        rows_normed, rows_noise, rows_goal = pieces
        condition = jnp.dot(rows_normed, cond_w, preferred_element_type=jnp.float32)
        preact = condition[:, None, :] + jnp.einsum('rsn,nh->rsh', rows_noise.astype(jnp.float32), noise_w)
        activation = jax.nn.silu(preact).astype(jnp.bfloat16)
        act_wide = widen(activation)
        samples = jnp.einsum('rsh,hl->rsl', act_wide, latent_w)
        energies, slopes = energy_score(samples, rows_goal.astype(jnp.float32))
        slope_wide = widen(slopes)
        latent_part = jnp.einsum('rsh,rsl->hl', act_wide, slope_wide)
        backward = jnp.einsum('rsl,hl->rsh', slope_wide, latent_w)
        pre_grad = (backward * silu_slope(preact)).astype(jnp.bfloat16)
        pre_wide = widen(pre_grad)
        noise_part = jnp.einsum('rsn,rsh->nh', rows_noise.astype(jnp.float32), pre_wide)
        cond_slope = lax.optimization_barrier(jnp.sum(pre_wide, axis=1)).astype(jnp.bfloat16)
        cond_part = jnp.dot(rows_normed.T, cond_slope, preferred_element_type=jnp.float32)
        return ((grads[0] + cond_part, grads[1] + noise_part, grads[2] + latent_part), energies)
    start_grads = (jnp.zeros((D, HW), jnp.float32), jnp.zeros((NZ, HW), jnp.float32), jnp.zeros((HW, LAT), jnp.float32))
    (cond_sum, noise_sum, latent_sum), energies = lax.scan(head_block, start_grads, inputs)
    squares_total = jnp.sum(cond_sum * cond_sum) + jnp.sum(noise_sum * noise_sum) + jnp.sum(latent_sum * latent_sum)
    rescale = lax.rsqrt(squares_total / (D * HW + NZ * HW + HW * LAT) + 1e-06)
    return (energies.reshape(POS), (cond_sum * rescale).astype(jnp.bfloat16), (noise_sum * rescale).astype(jnp.bfloat16), (latent_sum * rescale).astype(jnp.bfloat16))
```

```python
import jax
import jax.numpy as jnp
from jax import lax
from jax.sharding import Mesh
from jax.sharding import PartitionSpec as P

D = 4096
HW = 2048
LAT = 128
NZ = 128
S = 8
CHUNKS = 2

AXES = ("y", "zl", "core", "zh", "x")
NY, NZL, NC, NZH, NX = 4, 4, 2, 2, 4
f32, bf16 = jnp.float32, jnp.bfloat16


def pairs(move):
    out = []
    for y in range(NY):
        for zl in range(NZL):
            for c in range(NC):
                for zh in range(NZH):
                    for x in range(NX):
                        y2, zl2, c2, zh2, x2 = move(y, zl, c, zh, x)
                        src = (((y * NZL + zl) * NC + c) * NZH + zh) * NX + x
                        dst = (((y2 % NY) * NZL + zl2 % NZL) * NC + c2 % NC) * NZH + zh2 % NZH
                        out.append((src, dst * NX + x2 % NX))
    return out


def shift_x(k):
    return pairs(lambda y, zl, c, zh, x: (y, zl, c, zh, x + k))


def shift_y(k):
    return pairs(lambda y, zl, c, zh, x: (y + k, zl, c, zh, x))


def shift_z(k):
    def move(y, zl, c, zh, x):
        z = (zh * NZL + zl + k) % (NZH * NZL)
        return y, z % NZL, c, z // NZL, x

    return pairs(move)


def shift_zl(k):
    return pairs(lambda y, zl, c, zh, x: (y, zl + k, c, zh, x))


SWAP_CORE = pairs(lambda y, zl, c, zh, x: (y, zl, c + 1, zh, x))
RIGHT, LEFT = shift_x(1), shift_x(-1)
ACROSS = shift_z(4)


def send(value, plan):
    return lax.ppermute(value, AXES, plan)


def pick(array, index, axis=0):
    return lax.dynamic_index_in_dim(array, index, axis, keepdims=False)


def dot(left, right):
    return jnp.dot(left, right, preferred_element_type=f32)


def row_contract(left, right):
    return lax.dot_general(left, right, (((0,), (0,)), ((), ())), preferred_element_type=f32)


def by_place(pieces, place):
    count = len(pieces)
    out = jnp.zeros((count,) + pieces[0].shape, pieces[0].dtype)
    for s, piece in enumerate(pieces):
        out = lax.dynamic_update_index_in_dim(out, piece, (place - s) % count, 0)
    return out


def energy_score(samples, goal_rows):
    n_draws = samples.shape[1]
    diff_t = samples - goal_rows[:, None, :]
    dist_t = jnp.sqrt(jnp.sum(diff_t * diff_t, axis=-1) + 1.0)
    diff_p = samples[:, :, None, :] - samples[:, None, :, :]
    dist_p = jnp.sqrt(jnp.sum(diff_p * diff_p, axis=-1) + 1.0)
    off_diag = 1.0 - jnp.eye(n_draws, dtype=f32)
    pair_count = n_draws * (n_draws - 1)
    energies = jnp.mean(dist_t, axis=1) - jnp.sum(dist_p * off_diag, axis=(1, 2)) / (
        2.0 * pair_count
    )
    slopes = (
        diff_t / (n_draws * dist_t[..., None])
        - jnp.sum(diff_p / dist_p[..., None], axis=2) / pair_count
    )
    return energies, slopes.astype(bf16)


def silu_slope(values):
    sigmoid = jax.nn.sigmoid(values)
    return sigmoid * (1.0 + values * (1.0 - sigmoid))


def gather_other_block(block, y, core):
    rows = block.shape[0] // (NY * NC)
    share = lax.dynamic_slice_in_dim(block, (y * NC + core) * rows, rows, 0)
    mine = send(share, ACROSS)
    pieces = [mine, send(mine, shift_y(1)), send(mine, shift_y(2)), send(mine, shift_y(-1))]
    held = by_place(pieces, y)
    other = send(held, SWAP_CORE)
    first = jnp.where(core == 0, held, other)
    second = jnp.where(core == 0, other, held)
    return jnp.stack([first, second], axis=1).reshape(block.shape)


def reduce_rows(att, out_proj, residual, gain, zh, x, r):
    m = att.shape[2]
    half = D // 2
    sides = (out_proj[:, :half], out_proj[:, half:])

    def rows(step):
        mine = pick(pick(att, (x + step) % NX, 1), zh)
        other = pick(pick(att, (x + step) % NX, 1), 1 - zh)
        return jnp.concatenate([mine, other], axis=0)

    far, right, left, own = rows(2), rows(1), rows(3), rows(0)
    far_r = send(dot(far, sides[0]).astype(bf16), RIGHT)
    far_l = send(dot(far, sides[1]).astype(bf16), LEFT)
    from_l1 = send(dot(right, sides[1]).astype(bf16), RIGHT)
    from_r0 = send(dot(left, sides[0]).astype(bf16), LEFT)
    from_l0 = send((dot(right, sides[0]) + far_r.astype(f32)).astype(bf16), RIGHT)
    from_r1 = send((dot(left, sides[1]) + far_l.astype(f32)).astype(bf16), LEFT)
    hidden = []
    for side, a, b in ((0, from_l0, from_r0), (1, from_l1, from_r1)):
        total = dot(own, sides[side]) + a.astype(f32) + b.astype(f32)
        crossed = send(total[m:].astype(bf16), ACROSS)
        columns = slice(side * half, side * half + half)
        hidden.append(
            residual[r * m : r * m + m, columns].astype(f32) + total[:m] + crossed.astype(f32)
        )
    squares = sum(jnp.sum(h * h, axis=-1, keepdims=True) for h in hidden)
    scale = lax.rsqrt(squares / D + 1e-05)
    return [
        (h * scale * gain[i * half : i * half + half]).astype(bf16) for i, h in enumerate(hidden)
    ]


def gather_rows(halves):
    a, b = halves
    left = (send(a, RIGHT), send(b, RIGHT))
    right = (send(a, LEFT), send(b, LEFT))
    far = (send(left[0], RIGHT), send(right[1], LEFT))
    return [jnp.concatenate([h, left[i], right[i], far[i]], axis=0) for i, h in enumerate(halves)]


def reduce_samples(partial):
    own, left, right, far = partial
    h = far.shape[0] // 2
    far_r = send(far[:h], RIGHT)
    far_l = send(far[h:], LEFT)
    from_left = send(jnp.concatenate([right[:h] + far_r, right[h:]], axis=0), RIGHT)
    from_right = send(jnp.concatenate([left[:h], left[h:] + far_l], axis=0), LEFT)
    return own + from_left + from_right


def gather_slopes(own):
    h = own.shape[0] // 2
    left = send(own, RIGHT)
    right = send(own, LEFT)
    far_a = send(left[:h], RIGHT)
    far_b = send(right[h:], LEFT)
    return jnp.concatenate([own, left, right, far_a, far_b], axis=0)


def on_device(
    attended,
    out_proj,
    residual,
    norm_gain,
    cond_proj,
    noise_proj,
    latent_proj,
    noise_draws,
    targets,
):
    y, zl = lax.axis_index("y"), lax.axis_index("zl")
    core, zh, x = lax.axis_index("core"), lax.axis_index("zh"), lax.axis_index("x")
    n = CHUNKS
    m = residual.shape[0] // n
    width = cond_proj.shape[1]
    att = attended.reshape(NZH, NX, n, m, attended.shape[1])
    noise = pick(noise_draws.reshape(NZH, NX, n, m * S, NZ), zh)
    goals = targets.astype(f32)

    normed = [
        reduce_rows(att[:, :, r], out_proj, residual, norm_gain, zh, x, r) for r in range(n)
    ]
    cond_w = jnp.concatenate([cond_proj, gather_other_block(cond_proj, y, core)], axis=1)
    noise_w = jnp.concatenate([noise_proj, send(noise_proj, ACROSS)], axis=1)
    latent_w = jnp.concatenate([latent_proj, send(latent_proj, ACROSS)], axis=0)

    steps = []
    energies = []
    for r in range(n):
        rows = gather_rows(normed[r])
        condition = dot(rows[0], cond_w[: D // 2]) + dot(rows[1], cond_w[D // 2 :])
        draws = jnp.concatenate(
            [pick(noise, (x + step) % NX)[r] for step in (0, 3, 1, 2)], axis=0
        )
        preact = condition[:, None, :] + dot(draws, noise_w).reshape(NX * m, S, 2 * width)
        activation = jax.nn.silu(preact).astype(bf16).reshape(NX * m * S, 2 * width)
        partial = dot(activation, latent_w).reshape(NX, m * S, LAT)
        own = reduce_samples([partial[i] for i in range(NX)])
        energy, own_slopes = energy_score(own.reshape(m, S, LAT), goals[r * m : r * m + m])
        energies.append(energy)
        slopes = gather_slopes(own_slopes.reshape(m * S, LAT))
        backward = lax.dot_general(
            slopes, latent_w, (((1,), (1,)), ((), ())), preferred_element_type=f32
        ).reshape(preact.shape)
        pre_grad = (backward * silu_slope(preact)).astype(bf16)
        cond_slope = jnp.sum(pre_grad, axis=1, dtype=f32).astype(bf16)
        steps.append((rows, draws, activation, slopes, pre_grad.reshape(activation.shape), cond_slope))

    noise_part = sum(row_contract(s[1], s[4]) for s in steps)
    latent_part = sum(row_contract(s[3], s[2]) for s in steps)

    def share(second):
        blocks = []
        for b in range(NZH):
            columns = slice(b * width, b * width + width)
            cond_part = sum(
                row_contract(jnp.where(second, s[0][1], s[0][0]), s[5][:, columns]) for s in steps
            ).reshape(NY, NZL, -1, width)
            small = jnp.where(second, latent_part, noise_part)[:, columns]
            blocks.append(
                jnp.concatenate([cond_part, small.reshape(NY, NZL, -1, width)], axis=2)
            )
        return jnp.stack(blocks, axis=1)

    other_core = send(share(core == 0).astype(bf16), SWAP_CORE)
    held = share(core == 1) + other_core.astype(f32)

    total = pick(held, y)
    for step in (1, 2, 3):
        total = total + send(pick(held, (y + step) % NY).astype(bf16), shift_y(step)).astype(f32)
    place = zh * NZL + zl
    piece = pick(pick(total, 0), zl)
    for step in range(1, NZH * NZL):
        to = (place + step) % (NZH * NZL)
        part = pick(pick(total, (to // NZL + zh) % NZH), to % NZL)
        piece = piece + send(part.astype(bf16), shift_z(step)).astype(f32)

    squares_total = lax.psum(jnp.sum(piece * piece), AXES)
    rescale = lax.rsqrt(squares_total / (D * HW + NZ * HW + HW * LAT) + 1e-06)

    piece = piece.astype(bf16)
    quarter = by_place([piece] + [send(piece, shift_zl(s)) for s in (1, 2, 3)], zl)
    half = by_place([quarter] + [send(quarter, shift_y(s)) for s in (1, 2, 3)], y)
    other_half = send(half, SWAP_CORE)
    first = jnp.where(core == 0, half, other_half)
    second = jnp.where(core == 0, other_half, half)
    rows = D // (NC * NY * NZL)

    def scaled(value):
        return (value.astype(f32) * rescale).astype(bf16)

    cond_out = scaled(
        jnp.stack([first[:, :, :rows], second[:, :, :rows]], axis=0).reshape(D, width)
    )
    noise_out = scaled(first[:, :, rows:].reshape(NZ, width))
    latent_out = scaled(second[:, :, rows:].reshape(LAT, width).T)
    return (jnp.concatenate(energies), cond_out, noise_out, latent_out)


def solution(mesh):
    fine = Mesh(mesh.devices.reshape(NY, NZL, NC, NZH, NX), AXES)
    ctx, tp = ("y", "zl", "core"), ("zh", "x")
    return jax.shard_map(
        on_device,
        mesh=fine,
        in_specs=(
            P(ctx, tp),
            P(tp, None),
            P(AXES, None),
            P(),
            P(None, tp),
            P(None, tp),
            P(tp, None),
            P(ctx, None, None),
            P(AXES, None),
        ),
        out_specs=(P(AXES), P(None, tp), P(None, tp), P(tp, None)),
        check_vma=False,
    )
```

```python
import jax
import jax.numpy as jnp
from jax import lax
from jax.sharding import Mesh
from jax.sharding import PartitionSpec as P

D = 4096
HW = 2048
LAT = 128
NZ = 128
S = 8
CHUNKS = 2

AXES = ("y", "zl", "core", "zh", "x")
NY, NZL, NC, NZH, NX = 4, 4, 2, 2, 4
f32, bf16 = jnp.float32, jnp.bfloat16


def pairs(move):
    out = []
    for y in range(NY):
        for zl in range(NZL):
            for c in range(NC):
                for zh in range(NZH):
                    for x in range(NX):
                        y2, zl2, c2, zh2, x2 = move(y, zl, c, zh, x)
                        src = (((y * NZL + zl) * NC + c) * NZH + zh) * NX + x
                        dst = (((y2 % NY) * NZL + zl2 % NZL) * NC + c2 % NC) * NZH + zh2 % NZH
                        out.append((src, dst * NX + x2 % NX))
    return out


def shift_x(k):
    return pairs(lambda y, zl, c, zh, x: (y, zl, c, zh, x + k))


def shift_y(k):
    return pairs(lambda y, zl, c, zh, x: (y + k, zl, c, zh, x))


def shift_z(k):
    def move(y, zl, c, zh, x):
        z = (zh * NZL + zl + k) % (NZH * NZL)
        return y, z % NZL, c, z // NZL, x

    return pairs(move)


def shift_zl(k):
    return pairs(lambda y, zl, c, zh, x: (y, zl + k, c, zh, x))


SWAP_CORE = pairs(lambda y, zl, c, zh, x: (y, zl, c + 1, zh, x))
RIGHT, LEFT = shift_x(1), shift_x(-1)
ACROSS = shift_z(4)


def send(value, plan):
    return lax.ppermute(value, AXES, plan)


def pick(array, index, axis=0):
    return lax.dynamic_index_in_dim(array, index, axis, keepdims=False)


def dot(left, right):
    return jnp.dot(left, right, preferred_element_type=f32)


def row_contract(left, right):
    return lax.dot_general(left, right, (((0,), (0,)), ((), ())), preferred_element_type=f32)


def by_place(pieces, place):
    count = len(pieces)
    out = jnp.zeros((count,) + pieces[0].shape, pieces[0].dtype)
    for s, piece in enumerate(pieces):
        out = lax.dynamic_update_index_in_dim(out, piece, (place - s) % count, 0)
    return out


def energy_score(samples, goal_rows):
    n_draws = samples.shape[1]
    diff_t = samples - goal_rows[:, None, :]
    dist_t = jnp.sqrt(jnp.sum(diff_t * diff_t, axis=-1) + 1.0)
    diff_p = samples[:, :, None, :] - samples[:, None, :, :]
    dist_p = jnp.sqrt(jnp.sum(diff_p * diff_p, axis=-1) + 1.0)
    off_diag = 1.0 - jnp.eye(n_draws, dtype=f32)
    pair_count = n_draws * (n_draws - 1)
    energies = jnp.mean(dist_t, axis=1) - jnp.sum(dist_p * off_diag, axis=(1, 2)) / (
        2.0 * pair_count
    )
    slopes = (
        diff_t / (n_draws * dist_t[..., None])
        - jnp.sum(diff_p / dist_p[..., None], axis=2) / pair_count
    )
    return energies, slopes.astype(bf16)


def silu_slope(values):
    sigmoid = jax.nn.sigmoid(values)
    return sigmoid * (1.0 + values * (1.0 - sigmoid))


def after(value, *first):
    return lax.optimization_barrier((value,) + first)[0]


def project(att, out_proj, residual, norm_gain, zh, x, n):
    m = att.shape[3]
    half = D // 2

    def rows(step, r):
        block = pick(att[:, :, r], (x + step) % NX, 1)
        return jnp.concatenate([pick(block, zh), pick(block, 1 - zh)], axis=0)

    far = []
    for r in range(n):
        lhs = rows(2, r)
        if far:
            lhs = after(lhs, far[-1])
        far.append(dot(lhs, out_proj).astype(bf16))
    far_r = [send(f[:, :half], RIGHT) for f in far]
    far_l = [send(f[:, half:], LEFT) for f in far]
    marks, normed = [far[0]], []
    last = far[-1]
    for r in range(n):
        right, left = dot(after(rows(1, r), last), out_proj), dot(after(rows(3, r), last), out_proj)
        right = jnp.concatenate([right[:, :half] + far_r[r].astype(f32), right[:, half:]], axis=1)
        left = jnp.concatenate([left[:, :half], left[:, half:] + far_l[r].astype(f32)], axis=1)
        right, left = right.astype(bf16), left.astype(bf16)
        marks.append(left)
        from_left = send(right, RIGHT)
        from_right = send(left, LEFT)
        total = dot(rows(0, r), out_proj) + from_left.astype(f32) + from_right.astype(f32)
        crossed = send(total[m:].astype(bf16), ACROSS)
        if normed:
            crossed = after(crossed, normed[-1])
        h = residual[r * m : r * m + m].astype(f32) + total[:m] + crossed.astype(f32)
        scale = lax.rsqrt(jnp.mean(h * h, axis=-1, keepdims=True) + 1e-05)
        normed.append((h * scale * norm_gain).astype(bf16))
    return normed, marks


def gather_other_block(block, y, core, marks):
    rows = block.shape[0] // (NY * NC)
    share = lax.dynamic_slice_in_dim(block, (y * NC + core) * rows, rows, 0)
    mine = send(after(share, marks[0]), ACROSS)
    mine = after(mine, marks[1])
    pieces = [mine, send(mine, shift_y(1)), send(mine, shift_y(2)), send(mine, shift_y(3))]
    held = by_place(pieces, y)
    other = send(after(held, marks[2]), SWAP_CORE)
    first = jnp.where(core == 0, held, other)
    second = jnp.where(core == 0, other, held)
    return jnp.stack([first, second], axis=1).reshape(block.shape)


def gather_rows(own):
    half = D // 2
    left, right = send(own, RIGHT), send(own, LEFT)
    far = (send(left[:, :half], RIGHT), send(right[:, half:], LEFT))
    return [
        jnp.concatenate([part[:, i * half : i * half + half] for part in (own, left, right)] + [far[i]])
        for i in range(2)
    ]


def reduce_samples(partial):
    own, left, right, far = partial
    others = (
        send(far.astype(bf16), shift_x(2)),
        send(right.astype(bf16), RIGHT),
        send(left.astype(bf16), LEFT),
    )
    return own + sum(o.astype(f32) for o in others)


def gather_slopes(own):
    return jnp.concatenate(
        [own, send(own, RIGHT), send(own, LEFT), send(own, shift_x(2))], axis=0
    )


def butterfly(value, *plans):
    for plan in plans:
        value = value + send(value, plan)
    return value


def on_device(
    attended,
    out_proj,
    residual,
    norm_gain,
    cond_proj,
    noise_proj,
    latent_proj,
    noise_draws,
    targets,
):
    y, zl = lax.axis_index("y"), lax.axis_index("zl")
    core, zh, x = lax.axis_index("core"), lax.axis_index("zh"), lax.axis_index("x")
    n = CHUNKS
    m = residual.shape[0] // n
    width = cond_proj.shape[1]
    att = attended.reshape(NZH, NX, n, m, attended.shape[1])
    noise = pick(noise_draws.reshape(NZH, NX, n, m * S, NZ), zh)
    goals = targets.astype(f32)

    def both(block, other, axis):
        return jnp.concatenate(
            [jnp.where(zh == 0, block, other), jnp.where(zh == 0, other, block)], axis=axis
        )

    normed, marks = project(att, out_proj, residual, norm_gain, zh, x, n)
    cond_w = both(cond_proj, gather_other_block(cond_proj, y, core, marks), 1)
    noise_w = both(noise_proj, send(after(noise_proj, marks[1]), ACROSS), 1)
    latent_w = both(latent_proj, send(after(latent_proj, marks[1]), ACROSS), 0)

    grads = []
    energies = []
    for r in range(n):
        rows = gather_rows(normed[r])
        condition = dot(rows[0], cond_w[: D // 2]) + dot(rows[1], cond_w[D // 2 :])
        draws = jnp.concatenate(
            [pick(noise, (x + step) % NX)[r] for step in (0, 3, 1, 2)], axis=0
        )
        preact = condition[:, None, :] + dot(draws, noise_w).reshape(NX * m, S, 2 * width)
        activation = jax.nn.silu(preact).astype(bf16).reshape(NX * m * S, 2 * width)
        partial = dot(activation, latent_w).reshape(NX, m * S, LAT)
        own = reduce_samples([partial[i] for i in range(NX)])
        energy, own_slopes = energy_score(own.reshape(m, S, LAT), goals[r * m : r * m + m])
        energies.append(energy)
        slopes = gather_slopes(own_slopes.reshape(m * S, LAT))
        if grads:
            slopes = after(slopes, *grads[-1])
        backward = lax.dot_general(
            slopes, latent_w, (((1,), (1,)), ((), ())), preferred_element_type=f32
        ).reshape(preact.shape)
        pre_grad = (backward * silu_slope(preact)).astype(bf16)
        cond_slope = jnp.sum(pre_grad, axis=1, dtype=f32).astype(bf16)
        grads.append(
            (
                row_contract(draws, pre_grad.reshape(activation.shape)),
                row_contract(slopes, activation),
            )
            + tuple(
                row_contract(
                    jnp.where(second, rows[1], rows[0]),
                    cond_slope[:, b * width : b * width + width],
                )
                for second in (core == 0, core == 1)
                for b in range(NZH)
            )
        )

    sums = [sum(parts) for parts in zip(*grads)]

    def share(second, cond_parts):
        blocks = []
        for b, cond_part in enumerate(cond_parts):
            small = jnp.where(second, sums[1], sums[0])[:, b * width : b * width + width]
            blocks.append(
                jnp.concatenate(
                    [
                        cond_part.reshape(NY, NZL, -1, width),
                        small.reshape(NY, NZL, -1, width),
                    ],
                    axis=2,
                )
            )
        return jnp.stack(blocks, axis=1)

    other_core = send(share(core == 0, sums[2:4]).astype(bf16), SWAP_CORE)
    held = share(core == 1, sums[4:6]) + other_core.astype(f32)

    total = pick(held, y)
    for step in (1, 2, 3):
        total = total + send(pick(held, (y + step) % NY).astype(bf16), shift_y(step)).astype(f32)
    place = zh * NZL + zl
    piece = pick(pick(total, zh), zl)
    for step in range(1, NZH * NZL):
        to = (place + step) % (NZH * NZL)
        part = pick(pick(total, to // NZL), to % NZL)
        piece = piece + send(part.astype(bf16), shift_z(step)).astype(f32)

    piece = piece.astype(bf16)
    quarter = by_place([piece] + [send(piece, shift_zl(s)) for s in (1, 2, 3)], zl)
    sent = [send(quarter, shift_y(s)) for s in (1, 2, 3)]
    squares = jnp.square(quarter.astype(f32)).reshape(-1, 8, 2, 128)
    squares = butterfly(
        jnp.sum(squares, axis=(0, 2)),
        pairs(lambda y, zl, c, zh, x: (y, zl, c, zh, x ^ 1)),
        pairs(lambda y, zl, c, zh, x: (y, zl, c, zh, x ^ 2)),
        pairs(lambda y, zl, c, zh, x: (y ^ 1, zl, c, zh, x)),
        pairs(lambda y, zl, c, zh, x: (y ^ 2, zl, c, zh, x)),
    )
    *sent, squares = lax.optimization_barrier((*sent, squares))
    half = by_place([quarter] + sent, y)
    other_half = send(half, SWAP_CORE)
    squares = butterfly(squares, ACROSS, SWAP_CORE)
    rescale = lax.rsqrt(jnp.sum(squares) / (D * HW + NZ * HW + HW * LAT) + 1e-06)
    other_half, rescale = lax.optimization_barrier((other_half, rescale))
    first = jnp.where(core == 0, half, other_half)
    second = jnp.where(core == 0, other_half, half)
    rows = D // (NC * NY * NZL)

    def scaled(value):
        return (value.astype(f32) * rescale).astype(bf16)

    cond_out = scaled(
        jnp.stack([first[:, :, :rows], second[:, :, :rows]], axis=0).reshape(D, width)
    )
    noise_out = scaled(first[:, :, rows:].reshape(NZ, width))
    latent_out = scaled(second[:, :, rows:].reshape(LAT, width).T)
    return (jnp.concatenate(energies), cond_out, noise_out, latent_out)


def solution(mesh):
    fine = Mesh(mesh.devices.reshape(NY, NZL, NC, NZH, NX), AXES)
    ctx, tp = ("y", "zl", "core"), ("zh", "x")
    return jax.shard_map(
        on_device,
        mesh=fine,
        in_specs=(
            P(ctx, tp),
            P(tp, None),
            P(AXES, None),
            P(),
            P(None, tp),
            P(None, tp),
            P(tp, None),
            P(ctx, None, None),
            P(AXES, None),
        ),
        out_specs=(P(AXES), P(None, tp), P(None, tp), P(tp, None)),
        check_vma=False,
    )
```

```python
import jax
import jax.numpy as jnp
from jax import lax
from jax.sharding import Mesh
from jax.sharding import PartitionSpec as P

D = 4096
HW = 2048
LAT = 128
NZ = 128
S = 8
CHUNKS = 2
PIECES = 4

AXES = ("y", "zl", "core", "zh", "x")
NY, NZL, NC, NZH, NX = 4, 4, 2, 2, 4
f32, bf16 = jnp.float32, jnp.bfloat16


def pairs(move):
    out = []
    for y in range(NY):
        for zl in range(NZL):
            for c in range(NC):
                for zh in range(NZH):
                    for x in range(NX):
                        y2, zl2, c2, zh2, x2 = move(y, zl, c, zh, x)
                        src = (((y * NZL + zl) * NC + c) * NZH + zh) * NX + x
                        dst = (((y2 % NY) * NZL + zl2 % NZL) * NC + c2 % NC) * NZH + zh2 % NZH
                        out.append((src, dst * NX + x2 % NX))
    return out


def shift_x(k):
    return pairs(lambda y, zl, c, zh, x: (y, zl, c, zh, x + k))


def shift_y(k):
    return pairs(lambda y, zl, c, zh, x: (y + k, zl, c, zh, x))


def shift_z(k):
    def move(y, zl, c, zh, x):
        z = (zh * NZL + zl + k) % (NZH * NZL)
        return y, z % NZL, c, z // NZL, x

    return pairs(move)


def shift_zl(k):
    return pairs(lambda y, zl, c, zh, x: (y, zl + k, c, zh, x))


SWAP_CORE = pairs(lambda y, zl, c, zh, x: (y, zl, c + 1, zh, x))
RIGHT, LEFT = shift_x(1), shift_x(-1)
ACROSS = shift_z(4)


def send(value, plan):
    return lax.ppermute(value, AXES, plan)


def pick(array, index, axis=0):
    return lax.dynamic_index_in_dim(array, index, axis, keepdims=False)


def dot(left, right):
    return jnp.dot(left, right, preferred_element_type=f32)


def row_contract(left, right):
    return lax.dot_general(left, right, (((0,), (0,)), ((), ())), preferred_element_type=f32)


def by_place(pieces, place):
    count = len(pieces)
    out = jnp.zeros((count,) + pieces[0].shape, pieces[0].dtype)
    for s, piece in enumerate(pieces):
        out = lax.dynamic_update_index_in_dim(out, piece, (place - s) % count, 0)
    return out


def energy_score(samples, goal_rows):
    n_draws = samples.shape[1]
    diff_t = samples - goal_rows[:, None, :]
    dist_t = jnp.sqrt(jnp.sum(diff_t * diff_t, axis=-1) + 1.0)
    diff_p = samples[:, :, None, :] - samples[:, None, :, :]
    dist_p = jnp.sqrt(jnp.sum(diff_p * diff_p, axis=-1) + 1.0)
    off_diag = 1.0 - jnp.eye(n_draws, dtype=f32)
    pair_count = n_draws * (n_draws - 1)
    energies = jnp.mean(dist_t, axis=1) - jnp.sum(dist_p * off_diag, axis=(1, 2)) / (
        2.0 * pair_count
    )
    slopes = (
        diff_t / (n_draws * dist_t[..., None])
        - jnp.sum(diff_p / dist_p[..., None], axis=2) / pair_count
    )
    return energies, slopes.astype(bf16)


def silu_slope(values):
    sigmoid = jax.nn.sigmoid(values)
    return sigmoid * (1.0 + values * (1.0 - sigmoid))


def after(value, *first):
    return lax.optimization_barrier((value,) + first)[0]


def project(att, out_proj, residual, norm_gain, zh, x, n):
    pieces, m = att.shape[2:4]
    half = D // 2
    w0, w1 = out_proj[:, :half], out_proj[:, half:]

    def rows(step, r, *first):
        block = pick(att[:, :, r], (x + step) % NX, 1)
        both = jnp.concatenate([pick(block, zh), pick(block, 1 - zh)], axis=0)
        return after(both, *first) if first else both

    far, plain = [], []
    for r in range(pieces):
        lhs = rows(2, r, *(plain[-1] if plain else ()))
        far.append((dot(lhs, w0).astype(bf16), dot(lhs, w1).astype(bf16)))
        plain.append(
            (
                dot(rows(1, r, *far[-1]), w1).astype(bf16),
                dot(rows(3, r, *far[-1]), w0).astype(bf16),
            )
        )
    far = [(send(a, RIGHT), send(b, LEFT)) for a, b in far]
    got_plain = [(send(a, RIGHT), send(b, LEFT)) for a, b in plain]
    added = []
    for r in range(pieces):
        first = plain[min(r + 1, pieces - 1)] + (added[-1] if added else ())
        added.append(
            (
                (dot(rows(1, r, *first), w0) + far[r][0].astype(f32)).astype(bf16),
                (dot(rows(3, r, *first), w1) + far[r][1].astype(f32)).astype(bf16),
            )
        )
    got_added = [(send(a, RIGHT), send(b, LEFT)) for a, b in added]
    normed = []
    group = pieces // n
    for r in range(n):
        hidden = []
        for p in range(r * group, r * group + group):
            own = rows(0, p, *added[p])
            total = jnp.concatenate(
                [
                    dot(own, w0) + got_added[p][0].astype(f32) + got_plain[p][1].astype(f32),
                    dot(own, w1) + got_plain[p][0].astype(f32) + got_added[p][1].astype(f32),
                ],
                axis=1,
            )
            out = total[m:].astype(bf16)
            if normed:
                out = after(out, normed[-1])
            hidden.append(
                residual[p * m : p * m + m].astype(f32)
                + total[:m]
                + send(out, ACROSS).astype(f32)
            )
        h = jnp.concatenate(hidden)
        scale = lax.rsqrt(jnp.mean(h * h, axis=-1, keepdims=True) + 1e-05)
        normed.append((h * scale * norm_gain).astype(bf16))
    normed[0] = after(normed[0], *added[-1])
    return normed, (plain[0][0], added[0][0], added[2][0], added[3][0])


def gather_other_block(block, y, core, marks):
    rows = block.shape[0] // (NY * NC)
    share = lax.dynamic_slice_in_dim(block, (y * NC + core) * rows, rows, 0)
    mine = send(after(share, marks[0]), ACROSS)
    mine = after(mine, marks[1])
    pieces = [mine, send(mine, shift_y(1)), send(mine, shift_y(2)), send(mine, shift_y(3))]
    held = by_place(pieces, y)
    other = send(after(held, marks[2]), SWAP_CORE)
    first = jnp.where(core == 0, held, other)
    second = jnp.where(core == 0, other, held)
    return jnp.stack([first, second], axis=1).reshape(block.shape)


def gather_rows(own):
    half = D // 2
    left, right = send(own, RIGHT), send(own, LEFT)
    far = (send(left[:, :half], RIGHT), send(right[:, half:], LEFT))
    return [
        jnp.concatenate([part[:, i * half : i * half + half] for part in (own, left, right)] + [far[i]])
        for i in range(2)
    ]


def reduce_samples(partial):
    own, left, right, far = partial
    others = (
        send(far.astype(bf16), shift_x(2)),
        send(right.astype(bf16), RIGHT),
        send(left.astype(bf16), LEFT),
    )
    return own + sum(o.astype(f32) for o in others)


def gather_slopes(own):
    return jnp.concatenate(
        [own, send(own, RIGHT), send(own, LEFT), send(own, shift_x(2))], axis=0
    )


def add_by_two(value, first, second):
    def flip(move):
        return send(value, pairs(move))

    one, two = flip(first), flip(second)
    both = flip(lambda *place: first(*second(*place)))
    return (value + one) + (two + both)


def on_device(
    attended,
    out_proj,
    residual,
    norm_gain,
    cond_proj,
    noise_proj,
    latent_proj,
    noise_draws,
    targets,
):
    y, zl = lax.axis_index("y"), lax.axis_index("zl")
    core, zh, x = lax.axis_index("core"), lax.axis_index("zh"), lax.axis_index("x")
    n = CHUNKS
    m = residual.shape[0] // n
    width = cond_proj.shape[1]
    att = attended.reshape(NZH, NX, PIECES, -1, attended.shape[1])
    noise = pick(noise_draws.reshape(NZH, NX, n, m * S, NZ), zh)
    goals = targets.astype(f32)

    def both(block, other, axis):
        return jnp.concatenate(
            [jnp.where(zh == 0, block, other), jnp.where(zh == 0, other, block)], axis=axis
        )

    normed, marks = project(att, out_proj, residual, norm_gain, zh, x, n)
    cond_w = both(cond_proj, gather_other_block(cond_proj, y, core, marks), 1)
    noise_w = both(noise_proj, send(after(noise_proj, marks[3]), ACROSS), 1)
    latent_w = both(latent_proj, send(after(latent_proj, marks[3]), ACROSS), 0)

    grads = []
    energies = []
    for r in range(n):
        rows = gather_rows(normed[r])
        condition = dot(rows[0], cond_w[: D // 2]) + dot(rows[1], cond_w[D // 2 :])
        draws = jnp.concatenate(
            [pick(noise, (x + step) % NX)[r] for step in (0, 3, 1, 2)], axis=0
        )
        preact = condition[:, None, :] + dot(draws, noise_w).reshape(NX * m, S, 2 * width)
        activation = jax.nn.silu(preact).astype(bf16).reshape(NX * m * S, 2 * width)
        partial = dot(activation, latent_w).reshape(NX, m * S, LAT)
        own = reduce_samples([partial[i] for i in range(NX)])
        if r:
            own = after(own, own_slopes)
        energy, own_slopes = energy_score(own.reshape(m, S, LAT), goals[r * m : r * m + m])
        energies.append(energy)
        slopes = gather_slopes(own_slopes.reshape(m * S, LAT))
        if grads:
            slopes = after(slopes, *grads[-1])
        backward = lax.dot_general(
            slopes, latent_w, (((1,), (1,)), ((), ())), preferred_element_type=f32
        ).reshape(preact.shape)
        pre_grad = (backward * silu_slope(preact)).astype(bf16)
        cond_slope = jnp.sum(pre_grad, axis=1, dtype=f32).astype(bf16)
        grads.append(
            (
                row_contract(draws, pre_grad.reshape(activation.shape)),
                row_contract(slopes, activation),
            )
            + tuple(
                row_contract(
                    jnp.where(second, rows[1], rows[0]),
                    cond_slope[:, b * width : b * width + width],
                )
                for second in (core == 0, core == 1)
                for b in range(NZH)
            )
        )

    sums = [sum(parts) for parts in zip(*grads)]

    def share(second, cond_parts):
        blocks = []
        for b, cond_part in enumerate(cond_parts):
            small = jnp.where(second, sums[1], sums[0])[:, b * width : b * width + width]
            blocks.append(
                jnp.concatenate(
                    [
                        cond_part.reshape(NY, NZL, -1, width),
                        small.reshape(NY, NZL, -1, width),
                    ],
                    axis=2,
                )
            )
        return jnp.stack(blocks, axis=1)

    other_core = send(share(core == 0, sums[2:4]).astype(bf16), SWAP_CORE)
    held = share(core == 1, sums[4:6]) + other_core.astype(f32)

    total = pick(held, y)
    for step in (1, 2, 3):
        total = total + send(pick(held, (y + step) % NY).astype(bf16), shift_y(step)).astype(f32)
    place = zh * NZL + zl
    piece = pick(pick(total, zh), zl)
    for step in range(1, NZH * NZL):
        to = (place + step) % (NZH * NZL)
        part = pick(pick(total, to // NZL), to % NZL)
        piece = piece + send(part.astype(bf16), shift_z(step)).astype(f32)

    piece = piece.astype(bf16)
    quarter = by_place([piece] + [send(piece, shift_zl(s)) for s in (1, 2, 3)], zl)
    sent = [send(quarter, shift_y(s)) for s in (1, 2, 3)]
    squares = jnp.square(quarter.astype(f32)).reshape(-1, 8, 2, 128)
    squares = jnp.sum(squares, axis=(0, 2))
    squares = add_by_two(
        squares,
        lambda y, zl, c, zh, x: (y, zl, c, zh, x ^ 1),
        lambda y, zl, c, zh, x: (y, zl, c, zh, x ^ 2),
    )
    squares = add_by_two(
        squares,
        lambda y, zl, c, zh, x: (y ^ 1, zl, c, zh, x),
        lambda y, zl, c, zh, x: (y ^ 2, zl, c, zh, x),
    )
    squares = add_by_two(
        squares,
        lambda y, zl, c, zh, x: (y, zl, c ^ 1, zh, x),
        lambda y, zl, c, zh, x: (y, zl, c, zh ^ 1, x),
    )
    *sent, squares = lax.optimization_barrier((*sent, squares))
    half = by_place([quarter] + sent, y)
    other_half = send(half, SWAP_CORE)
    rescale = lax.rsqrt(jnp.sum(squares) / (D * HW + NZ * HW + HW * LAT) + 1e-06)
    first = jnp.where(core == 0, half, other_half)
    second = jnp.where(core == 0, other_half, half)
    rows = D // (NC * NY * NZL)

    def scaled(value):
        return (value.astype(f32) * rescale).astype(bf16)

    cond_out = scaled(
        jnp.stack([first[:, :, :rows], second[:, :, :rows]], axis=0).reshape(D, width)
    )
    noise_out = scaled(first[:, :, rows:].reshape(NZ, width))
    latent_out = scaled(second[:, :, rows:].reshape(LAT, width).T)
    return (jnp.concatenate(energies), cond_out, noise_out, latent_out)


def solution(mesh):
    fine = Mesh(mesh.devices.reshape(NY, NZL, NC, NZH, NX), AXES)
    ctx, tp = ("y", "zl", "core"), ("zh", "x")
    return jax.shard_map(
        on_device,
        mesh=fine,
        in_specs=(
            P(ctx, tp),
            P(tp, None),
            P(AXES, None),
            P(),
            P(None, tp),
            P(None, tp),
            P(tp, None),
            P(ctx, None, None),
            P(AXES, None),
        ),
        out_specs=(P(AXES), P(None, tp), P(None, tp), P(tp, None)),
        check_vma=False,
    )
```

```python
import jax
import jax.numpy as jnp
from jax import lax
from jax.sharding import Mesh
from jax.sharding import PartitionSpec as P

D = 4096
HW = 2048
LAT = 128
NZ = 128
S = 8
CHUNKS = 2

AXES = ("y", "zl", "core", "zh", "x")
NY, NZL, NC, NZH, NX = 4, 4, 2, 2, 4
f32, bf16 = jnp.float32, jnp.bfloat16


def pairs(move):
    out = []
    for y in range(NY):
        for zl in range(NZL):
            for c in range(NC):
                for zh in range(NZH):
                    for x in range(NX):
                        y2, zl2, c2, zh2, x2 = move(y, zl, c, zh, x)
                        src = (((y * NZL + zl) * NC + c) * NZH + zh) * NX + x
                        dst = (((y2 % NY) * NZL + zl2 % NZL) * NC + c2 % NC) * NZH + zh2 % NZH
                        out.append((src, dst * NX + x2 % NX))
    return out


def shift_x(k):
    return pairs(lambda y, zl, c, zh, x: (y, zl, c, zh, x + k))


def shift_y(k):
    return pairs(lambda y, zl, c, zh, x: (y + k, zl, c, zh, x))


def shift_z(k):
    def move(y, zl, c, zh, x):
        z = (zh * NZL + zl + k) % (NZH * NZL)
        return y, z % NZL, c, z // NZL, x

    return pairs(move)


def shift_zl(k):
    return pairs(lambda y, zl, c, zh, x: (y, zl + k, c, zh, x))


SWAP_CORE = pairs(lambda y, zl, c, zh, x: (y, zl, c + 1, zh, x))
RIGHT, LEFT = shift_x(1), shift_x(-1)
ACROSS = shift_z(4)


def send(value, plan):
    return lax.ppermute(value, AXES, plan)


def pick(array, index, axis=0):
    return lax.dynamic_index_in_dim(array, index, axis, keepdims=False)


def dot(left, right):
    return jnp.dot(left, right, preferred_element_type=f32)


def row_contract(left, right):
    return lax.dot_general(left, right, (((0,), (0,)), ((), ())), preferred_element_type=f32)


def by_place(pieces, place):
    count = len(pieces)
    out = jnp.zeros((count,) + pieces[0].shape, pieces[0].dtype)
    for s, piece in enumerate(pieces):
        out = lax.dynamic_update_index_in_dim(out, piece, (place - s) % count, 0)
    return out


def energy_score(samples, goal_rows):
    n_draws = samples.shape[1]
    diff_t = samples - goal_rows[:, None, :]
    dist_t = jnp.sqrt(jnp.sum(diff_t * diff_t, axis=-1) + 1.0)
    diff_p = samples[:, :, None, :] - samples[:, None, :, :]
    dist_p = jnp.sqrt(jnp.sum(diff_p * diff_p, axis=-1) + 1.0)
    off_diag = 1.0 - jnp.eye(n_draws, dtype=f32)
    pair_count = n_draws * (n_draws - 1)
    energies = jnp.mean(dist_t, axis=1) - jnp.sum(dist_p * off_diag, axis=(1, 2)) / (
        2.0 * pair_count
    )
    slopes = (
        diff_t / (n_draws * dist_t[..., None])
        - jnp.sum(diff_p / dist_p[..., None], axis=2) / pair_count
    )
    return energies, slopes.astype(bf16)


def silu_slope(values):
    sigmoid = jax.nn.sigmoid(values)
    return sigmoid * (1.0 + values * (1.0 - sigmoid))


def after(value, *first):
    return lax.optimization_barrier((value,) + first)[0]


def project(att, out_proj, residual, norm_gain, zh, x, n):
    m = att.shape[3]
    half = D // 2

    def rows(step, r):
        block = pick(att[:, :, r], (x + step) % NX, 1)
        return jnp.concatenate([pick(block, zh), pick(block, 1 - zh)], axis=0)

    w0, w1 = out_proj[:, :half], out_proj[:, half:]
    far, plain = [], []
    for r in range(n):
        lhs = rows(2, r)
        if far:
            lhs = after(lhs, *far[-1])
        far.append((dot(lhs, w0).astype(bf16), dot(lhs, w1).astype(bf16)))
    for r in range(n):
        plain.append(
            (
                dot(after(rows(1, r), *far[-1]), w1).astype(bf16),
                dot(after(rows(3, r), *far[-1]), w0).astype(bf16),
            )
        )
    far = [(send(a, RIGHT), send(b, LEFT)) for a, b in far]
    marks, normed = [plain[0][0]], []
    for r in range(n):
        right = (dot(rows(1, r), w0) + far[r][0].astype(f32)).astype(bf16)
        left = (dot(rows(3, r), w1) + far[r][1].astype(f32)).astype(bf16)
        right = jnp.concatenate([right, plain[r][0]], axis=1)
        left = jnp.concatenate([plain[r][1], left], axis=1)
        marks.append(left)
        from_left = send(right, RIGHT)
        from_right = send(left, LEFT)
        total = dot(rows(0, r), out_proj) + from_left.astype(f32) + from_right.astype(f32)
        out = total[m:].astype(bf16)
        if normed:
            out = after(out, normed[-1])
        crossed = send(out, ACROSS)
        h = residual[r * m : r * m + m].astype(f32) + total[:m] + crossed.astype(f32)
        scale = lax.rsqrt(jnp.mean(h * h, axis=-1, keepdims=True) + 1e-05)
        normed.append((h * scale * norm_gain).astype(bf16))
    return normed, marks


def gather_other_block(block, y, core, marks):
    rows = block.shape[0] // (NY * NC)
    share = lax.dynamic_slice_in_dim(block, (y * NC + core) * rows, rows, 0)
    mine = send(after(share, marks[0]), ACROSS)
    mine = after(mine, marks[1])
    pieces = [mine, send(mine, shift_y(1)), send(mine, shift_y(2)), send(mine, shift_y(3))]
    held = by_place(pieces, y)
    other = send(after(held, marks[2]), SWAP_CORE)
    first = jnp.where(core == 0, held, other)
    second = jnp.where(core == 0, other, held)
    return jnp.stack([first, second], axis=1).reshape(block.shape)


def gather_rows(own):
    half = D // 2
    left, right = send(own, RIGHT), send(own, LEFT)
    far = (send(left[:, :half], RIGHT), send(right[:, half:], LEFT))
    return [
        jnp.concatenate([part[:, i * half : i * half + half] for part in (own, left, right)] + [far[i]])
        for i in range(2)
    ]


def reduce_samples(partial):
    own, left, right, far = partial
    others = (
        send(far.astype(bf16), shift_x(2)),
        send(right.astype(bf16), RIGHT),
        send(left.astype(bf16), LEFT),
    )
    return own + sum(o.astype(f32) for o in others)


def gather_slopes(own):
    return jnp.concatenate(
        [own, send(own, RIGHT), send(own, LEFT), send(own, shift_x(2))], axis=0
    )


def butterfly(value, *plans):
    for plan in plans:
        value = value + send(value, plan)
    return value


def on_device(
    attended,
    out_proj,
    residual,
    norm_gain,
    cond_proj,
    noise_proj,
    latent_proj,
    noise_draws,
    targets,
):
    y, zl = lax.axis_index("y"), lax.axis_index("zl")
    core, zh, x = lax.axis_index("core"), lax.axis_index("zh"), lax.axis_index("x")
    n = CHUNKS
    m = residual.shape[0] // n
    width = cond_proj.shape[1]
    att = attended.reshape(NZH, NX, n, m, attended.shape[1])
    noise = pick(noise_draws.reshape(NZH, NX, n, m * S, NZ), zh)
    goals = targets.astype(f32)

    def both(block, other, axis):
        return jnp.concatenate(
            [jnp.where(zh == 0, block, other), jnp.where(zh == 0, other, block)], axis=axis
        )

    normed, marks = project(att, out_proj, residual, norm_gain, zh, x, n)
    cond_w = both(cond_proj, gather_other_block(cond_proj, y, core, marks), 1)
    noise_w = both(noise_proj, send(after(noise_proj, marks[2]), ACROSS), 1)
    latent_w = both(latent_proj, send(after(latent_proj, marks[2]), ACROSS), 0)

    grads = []
    energies = []
    for r in range(n):
        rows = gather_rows(normed[r])
        condition = dot(rows[0], cond_w[: D // 2]) + dot(rows[1], cond_w[D // 2 :])
        draws = jnp.concatenate(
            [pick(noise, (x + step) % NX)[r] for step in (0, 3, 1, 2)], axis=0
        )
        preact = condition[:, None, :] + dot(draws, noise_w).reshape(NX * m, S, 2 * width)
        activation = jax.nn.silu(preact).astype(bf16).reshape(NX * m * S, 2 * width)
        if r:
            activation = after(activation, own_slopes)
        partial = dot(activation, latent_w).reshape(NX, m * S, LAT)
        own = reduce_samples([partial[i] for i in range(NX)])
        if r:
            own = after(own, pre_grad)
        energy, own_slopes = energy_score(own.reshape(m, S, LAT), goals[r * m : r * m + m])
        energies.append(energy)
        slopes = gather_slopes(own_slopes.reshape(m * S, LAT))
        if grads:
            slopes = after(slopes, *grads[-1])
        backward = lax.dot_general(
            slopes, latent_w, (((1,), (1,)), ((), ())), preferred_element_type=f32
        ).reshape(preact.shape)
        pre_grad = (backward * silu_slope(preact)).astype(bf16)
        cond_slope = jnp.sum(pre_grad, axis=1, dtype=f32).astype(bf16)
        grads.append(
            (
                row_contract(draws, pre_grad.reshape(activation.shape)),
                row_contract(slopes, activation),
            )
            + tuple(
                row_contract(
                    jnp.where(second, rows[1], rows[0]),
                    cond_slope[:, b * width : b * width + width],
                )
                for second in (core == 0, core == 1)
                for b in range(NZH)
            )
        )

    sums = [sum(parts) for parts in zip(*grads)]

    def share(second, cond_parts):
        blocks = []
        for b, cond_part in enumerate(cond_parts):
            small = jnp.where(second, sums[1], sums[0])[:, b * width : b * width + width]
            blocks.append(
                jnp.concatenate(
                    [
                        cond_part.reshape(NY, NZL, -1, width),
                        small.reshape(NY, NZL, -1, width),
                    ],
                    axis=2,
                )
            )
        return jnp.stack(blocks, axis=1)

    other_core = send(share(core == 0, sums[2:4]).astype(bf16), SWAP_CORE)
    held = share(core == 1, sums[4:6]) + other_core.astype(f32)

    total = pick(held, y)
    for step in (1, 2, 3):
        total = total + send(pick(held, (y + step) % NY).astype(bf16), shift_y(step)).astype(f32)
    place = zh * NZL + zl
    piece = pick(pick(total, zh), zl)
    for step in range(1, NZH * NZL):
        to = (place + step) % (NZH * NZL)
        part = pick(pick(total, to // NZL), to % NZL)
        piece = piece + send(part.astype(bf16), shift_z(step)).astype(f32)

    piece = piece.astype(bf16)
    quarter = by_place([piece] + [send(piece, shift_zl(s)) for s in (1, 2, 3)], zl)
    sent = [send(quarter, shift_y(s)) for s in (1, 2, 3)]
    squares = jnp.square(quarter.astype(f32)).reshape(-1, 8, 2, 128)
    squares = butterfly(
        jnp.sum(squares, axis=(0, 2)),
        ACROSS,
        pairs(lambda y, zl, c, zh, x: (y, zl, c, zh, x ^ 1)),
        pairs(lambda y, zl, c, zh, x: (y, zl, c, zh, x ^ 2)),
        pairs(lambda y, zl, c, zh, x: (y ^ 1, zl, c, zh, x)),
        pairs(lambda y, zl, c, zh, x: (y ^ 2, zl, c, zh, x)),
    )
    *sent, squares = lax.optimization_barrier((*sent, squares))
    half = by_place([quarter] + sent, y)
    other_half = send(half, SWAP_CORE)
    squares = butterfly(squares, SWAP_CORE)
    rescale = lax.rsqrt(jnp.sum(squares) / (D * HW + NZ * HW + HW * LAT) + 1e-06)
    other_half, rescale = lax.optimization_barrier((other_half, rescale))
    first = jnp.where(core == 0, half, other_half)
    second = jnp.where(core == 0, other_half, half)
    rows = D // (NC * NY * NZL)

    def scaled(value):
        return (value.astype(f32) * rescale).astype(bf16)

    cond_out = scaled(
        jnp.stack([first[:, :, :rows], second[:, :, :rows]], axis=0).reshape(D, width)
    )
    noise_out = scaled(first[:, :, rows:].reshape(NZ, width))
    latent_out = scaled(second[:, :, rows:].reshape(LAT, width).T)
    return (jnp.concatenate(energies), cond_out, noise_out, latent_out)


def solution(mesh):
    fine = Mesh(mesh.devices.reshape(NY, NZL, NC, NZH, NX), AXES)
    ctx, tp = ("y", "zl", "core"), ("zh", "x")
    return jax.shard_map(
        on_device,
        mesh=fine,
        in_specs=(
            P(ctx, tp),
            P(tp, None),
            P(AXES, None),
            P(),
            P(None, tp),
            P(None, tp),
            P(tp, None),
            P(ctx, None, None),
            P(AXES, None),
        ),
        out_specs=(P(AXES), P(None, tp), P(None, tp), P(tp, None)),
        check_vma=False,
    )
```

```python
import jax
import jax.numpy as jnp
from jax import lax
from jax.sharding import Mesh
from jax.sharding import PartitionSpec as P

D = 4096
HW = 2048
LAT = 128
NZ = 128
S = 8
CHUNKS = 2

AXES = ("y", "zl", "core", "zh", "x")
NY, NZL, NC, NZH, NX = 4, 4, 2, 2, 4
f32, bf16 = jnp.float32, jnp.bfloat16


def pairs(move):
    out = []
    for y in range(NY):
        for zl in range(NZL):
            for c in range(NC):
                for zh in range(NZH):
                    for x in range(NX):
                        y2, zl2, c2, zh2, x2 = move(y, zl, c, zh, x)
                        src = (((y * NZL + zl) * NC + c) * NZH + zh) * NX + x
                        dst = (((y2 % NY) * NZL + zl2 % NZL) * NC + c2 % NC) * NZH + zh2 % NZH
                        out.append((src, dst * NX + x2 % NX))
    return out


def shift_x(k):
    return pairs(lambda y, zl, c, zh, x: (y, zl, c, zh, x + k))


def shift_y(k):
    return pairs(lambda y, zl, c, zh, x: (y + k, zl, c, zh, x))


def shift_z(k):
    def move(y, zl, c, zh, x):
        z = (zh * NZL + zl + k) % (NZH * NZL)
        return y, z % NZL, c, z // NZL, x

    return pairs(move)


def shift_zl(k):
    return pairs(lambda y, zl, c, zh, x: (y, zl + k, c, zh, x))


SWAP_CORE = pairs(lambda y, zl, c, zh, x: (y, zl, c + 1, zh, x))
RIGHT, LEFT = shift_x(1), shift_x(-1)
ACROSS = shift_z(4)


def send(value, plan):
    return lax.ppermute(value, AXES, plan)


def pick(array, index, axis=0):
    return lax.dynamic_index_in_dim(array, index, axis, keepdims=False)


def dot(left, right):
    return jnp.dot(left, right, preferred_element_type=f32)


def row_contract(left, right):
    return lax.dot_general(left, right, (((0,), (0,)), ((), ())), preferred_element_type=f32)


def by_place(pieces, place):
    count = len(pieces)
    out = jnp.zeros((count,) + pieces[0].shape, pieces[0].dtype)
    for s, piece in enumerate(pieces):
        out = lax.dynamic_update_index_in_dim(out, piece, (place - s) % count, 0)
    return out


def energy_score(samples, goal_rows):
    n_draws = samples.shape[1]
    diff_t = samples - goal_rows[:, None, :]
    dist_t = jnp.sqrt(jnp.sum(diff_t * diff_t, axis=-1) + 1.0)
    diff_p = samples[:, :, None, :] - samples[:, None, :, :]
    dist_p = jnp.sqrt(jnp.sum(diff_p * diff_p, axis=-1) + 1.0)
    off_diag = 1.0 - jnp.eye(n_draws, dtype=f32)
    pair_count = n_draws * (n_draws - 1)
    energies = jnp.mean(dist_t, axis=1) - jnp.sum(dist_p * off_diag, axis=(1, 2)) / (
        2.0 * pair_count
    )
    slopes = (
        diff_t / (n_draws * dist_t[..., None])
        - jnp.sum(diff_p / dist_p[..., None], axis=2) / pair_count
    )
    return energies, slopes.astype(bf16)


def silu_slope(values):
    sigmoid = jax.nn.sigmoid(values)
    return sigmoid * (1.0 + values * (1.0 - sigmoid))


def after(value, *first):
    return lax.optimization_barrier((value,) + first)[0]


def project(att, out_proj, residual, norm_gain, zh, x, n):
    m = att.shape[3]
    half = D // 2

    def rows(step, r):
        block = pick(att[:, :, r], (x + step) % NX, 1)
        return jnp.concatenate([pick(block, zh), pick(block, 1 - zh)], axis=0)

    w0, w1 = out_proj[:, :half], out_proj[:, half:]
    far, plain = [], []
    for r in range(n):
        lhs = rows(2, r)
        if far:
            lhs = after(lhs, *far[-1])
        far.append((dot(lhs, w0).astype(bf16), dot(lhs, w1).astype(bf16)))
    for r in range(n):
        plain.append(
            (
                dot(after(rows(1, r), *far[-1]), w1).astype(bf16),
                dot(after(rows(3, r), *far[-1]), w0).astype(bf16),
            )
        )
    marks, normed = [far[0][1], plain[1][1]], []
    far = [(send(a, RIGHT), send(b, LEFT)) for a, b in far]
    first, waiting = plain[0], []
    for r in range(n):
        right = (dot(after(rows(1, r), *first), w0) + far[r][0].astype(f32)).astype(bf16)
        left = (dot(after(rows(3, r), *first), w1) + far[r][1].astype(f32)).astype(bf16)
        right = jnp.concatenate([right, plain[r][0]], axis=1)
        left = jnp.concatenate([plain[r][1], left], axis=1)
        first = (left,)
        marks.append(left)
        from_left = send(right, RIGHT)
        from_right = send(left, LEFT)
        total = dot(rows(0, r), out_proj) + from_left.astype(f32) + from_right.astype(f32)
        out = total[m:].astype(bf16)
        if normed:
            out = after(out, normed[-1])
        waiting.append((residual[r * m : r * m + m].astype(f32) + total[:m], send(out, ACROSS)))
        if not normed:
            normed.append(finish_rows(*waiting[0], norm_gain))
    return normed + waiting[1:], marks


def finish_rows(base, crossed, norm_gain):
    h = base + crossed.astype(f32)
    scale = lax.rsqrt(jnp.mean(h * h, axis=-1, keepdims=True) + 1e-05)
    return (h * scale * norm_gain).astype(bf16)


def other_weights(cond_proj, noise_proj, latent_proj, y, core, marks):
    width = cond_proj.shape[1]
    rows = cond_proj.shape[0] // (NY * NC)
    share = lax.dynamic_slice_in_dim(cond_proj, (y * NC + core) * rows, rows, 0)
    latent = jnp.concatenate([latent_proj[:LAT], latent_proj[LAT:]], axis=1)
    packed = jnp.concatenate([share, noise_proj, latent], axis=0)
    packed = after(send(after(packed, marks[0]), ACROSS), marks[1])
    mine, noise, latent = packed[:rows], packed[rows : rows + NZ], packed[rows + NZ :]
    pieces = [mine, send(mine, shift_y(1)), send(mine, shift_y(2)), send(mine, shift_y(3))]
    held = by_place(pieces, y)
    other = send(after(held, marks[2]), SWAP_CORE)
    first = jnp.where(core == 0, held, other)
    second = jnp.where(core == 0, other, held)
    return (
        jnp.stack([first, second], axis=1).reshape(cond_proj.shape),
        noise,
        jnp.concatenate([latent[:, :LAT], latent[:, LAT:]], axis=0),
    )


def gather_rows(own):
    half = D // 2
    left, right = send(own, RIGHT), send(own, LEFT)
    far = (send(left[:, :half], RIGHT), send(right[:, half:], LEFT))
    return [
        jnp.concatenate([part[:, i * half : i * half + half] for part in (own, left, right)] + [far[i]])
        for i in range(2)
    ]


def reduce_samples(partial):
    own, left, right, far = partial
    others = (
        send(far.astype(bf16), shift_x(2)),
        send(right.astype(bf16), RIGHT),
        send(left.astype(bf16), LEFT),
    )
    return own + sum(o.astype(f32) for o in others)


def gather_slopes(own):
    return jnp.concatenate(
        [own, send(own, RIGHT), send(own, LEFT), send(own, shift_x(2))], axis=0
    )


def butterfly(value, *plans):
    for plan in plans:
        value = value + send(value, plan)
    return value


def on_device(
    attended,
    out_proj,
    residual,
    norm_gain,
    cond_proj,
    noise_proj,
    latent_proj,
    noise_draws,
    targets,
):
    y, zl = lax.axis_index("y"), lax.axis_index("zl")
    core, zh, x = lax.axis_index("core"), lax.axis_index("zh"), lax.axis_index("x")
    n = CHUNKS
    m = residual.shape[0] // n
    width = cond_proj.shape[1]
    att = attended.reshape(NZH, NX, n, m, attended.shape[1])
    noise = pick(noise_draws.reshape(NZH, NX, n, m * S, NZ), zh)
    goals = targets.astype(f32)

    def both(block, other, axis):
        return jnp.concatenate(
            [jnp.where(zh == 0, block, other), jnp.where(zh == 0, other, block)], axis=axis
        )

    normed, marks = project(att, out_proj, residual, norm_gain, zh, x, n)
    other = other_weights(cond_proj, noise_proj, latent_proj, y, core, marks)
    cond_w = both(cond_proj, other[0], 1)
    noise_w = both(noise_proj, other[1], 1)
    latent_w = both(latent_proj, other[2], 0)

    grads = []
    energies = []
    for r in range(n):
        if r:
            normed[r] = finish_rows(normed[r][0], after(normed[r][1], partial), norm_gain)
        rows = gather_rows(normed[r])
        condition = dot(rows[0], cond_w[: D // 2]) + dot(rows[1], cond_w[D // 2 :])
        draws = jnp.concatenate(
            [pick(noise, (x + step) % NX)[r] for step in (0, 3, 1, 2)], axis=0
        )
        preact = condition[:, None, :] + dot(draws, noise_w).reshape(NX * m, S, 2 * width)
        activation = jax.nn.silu(preact).astype(bf16).reshape(NX * m * S, 2 * width)
        if r:
            activation = after(activation, own_slopes)
        partial = dot(activation, latent_w).reshape(NX, m * S, LAT)
        own = reduce_samples([partial[i] for i in range(NX)])
        if r:
            own = after(own, pre_grad)
        energy, own_slopes = energy_score(own.reshape(m, S, LAT), goals[r * m : r * m + m])
        energies.append(energy)
        slopes = gather_slopes(own_slopes.reshape(m * S, LAT))
        if grads:
            slopes = after(slopes, *grads[-1])
        backward = lax.dot_general(
            slopes, latent_w, (((1,), (1,)), ((), ())), preferred_element_type=f32
        ).reshape(preact.shape)
        pre_grad = (backward * silu_slope(preact)).astype(bf16)
        cond_slope = jnp.sum(pre_grad, axis=1, dtype=f32).astype(bf16)
        grads.append(
            (
                row_contract(draws, pre_grad.reshape(activation.shape)),
                row_contract(slopes, activation),
            )
            + tuple(
                row_contract(
                    jnp.where(second, rows[1], rows[0]),
                    cond_slope[:, b * width : b * width + width],
                )
                for second in (core == 0, core == 1)
                for b in range(NZH)
            )
        )

    sums = [sum(parts) for parts in zip(*grads)]

    def share(second, cond_parts):
        blocks = []
        for b, cond_part in enumerate(cond_parts):
            small = jnp.where(second, sums[1], sums[0])[:, b * width : b * width + width]
            blocks.append(
                jnp.concatenate(
                    [
                        cond_part.reshape(NY, NZL, -1, width),
                        small.reshape(NY, NZL, -1, width),
                    ],
                    axis=2,
                )
            )
        return jnp.stack(blocks, axis=1)

    other_core = send(share(core == 0, sums[2:4]).astype(bf16), SWAP_CORE)
    held = share(core == 1, sums[4:6]) + other_core.astype(f32)

    total = pick(held, y)
    for step in (1, 2, 3):
        total = total + send(pick(held, (y + step) % NY).astype(bf16), shift_y(step)).astype(f32)
    place = zh * NZL + zl
    piece = pick(pick(total, zh), zl)
    for step in range(1, NZH * NZL):
        to = (place + step) % (NZH * NZL)
        part = pick(pick(total, to // NZL), to % NZL)
        piece = piece + send(part.astype(bf16), shift_z(step)).astype(f32)

    piece = piece.astype(bf16)
    quarter = by_place([piece] + [send(piece, shift_zl(s)) for s in (1, 2, 3)], zl)
    sent = [send(quarter, shift_y(s)) for s in (1, 2, 3)]
    squares = jnp.square(quarter.astype(f32)).reshape(-1, 8, 2, 128)
    squares = butterfly(
        jnp.sum(squares, axis=(0, 2)),
        ACROSS,
        pairs(lambda y, zl, c, zh, x: (y, zl, c, zh, x ^ 1)),
        pairs(lambda y, zl, c, zh, x: (y, zl, c, zh, x ^ 2)),
        pairs(lambda y, zl, c, zh, x: (y ^ 1, zl, c, zh, x)),
        pairs(lambda y, zl, c, zh, x: (y ^ 2, zl, c, zh, x)),
    )
    *sent, squares = lax.optimization_barrier((*sent, squares))
    half = by_place([quarter] + sent, y)
    other_half = send(half, SWAP_CORE)
    squares = butterfly(squares, SWAP_CORE)
    rescale = lax.rsqrt(jnp.sum(squares) / (D * HW + NZ * HW + HW * LAT) + 1e-06)
    other_half, rescale = lax.optimization_barrier((other_half, rescale))
    first = jnp.where(core == 0, half, other_half)
    second = jnp.where(core == 0, other_half, half)
    rows = D // (NC * NY * NZL)

    def scaled(value):
        return (value.astype(f32) * rescale).astype(bf16)

    cond_out = scaled(
        jnp.stack([first[:, :, :rows], second[:, :, :rows]], axis=0).reshape(D, width)
    )
    noise_out = scaled(first[:, :, rows:].reshape(NZ, width))
    latent_out = scaled(second[:, :, rows:].reshape(LAT, width).T)
    return (jnp.concatenate(energies), cond_out, noise_out, latent_out)


def solution(mesh):
    fine = Mesh(mesh.devices.reshape(NY, NZL, NC, NZH, NX), AXES)
    ctx, tp = ("y", "zl", "core"), ("zh", "x")
    return jax.shard_map(
        on_device,
        mesh=fine,
        in_specs=(
            P(ctx, tp),
            P(tp, None),
            P(AXES, None),
            P(),
            P(None, tp),
            P(None, tp),
            P(tp, None),
            P(ctx, None, None),
            P(AXES, None),
        ),
        out_specs=(P(AXES), P(None, tp), P(None, tp), P(tp, None)),
        check_vma=False,
    )
```

```python
import jax
import jax.numpy as jnp
from jax import lax
from jax.sharding import Mesh
from jax.sharding import PartitionSpec as P

D = 4096
HW = 2048
LAT = 128
NZ = 128
S = 8
CHUNKS = 2

AXES = ("y", "zl", "core", "zh", "x")
NY, NZL, NC, NZH, NX = 4, 4, 2, 2, 4
f32, bf16 = jnp.float32, jnp.bfloat16


def pairs(move):
    out = []
    for y in range(NY):
        for zl in range(NZL):
            for c in range(NC):
                for zh in range(NZH):
                    for x in range(NX):
                        y2, zl2, c2, zh2, x2 = move(y, zl, c, zh, x)
                        src = (((y * NZL + zl) * NC + c) * NZH + zh) * NX + x
                        dst = (((y2 % NY) * NZL + zl2 % NZL) * NC + c2 % NC) * NZH + zh2 % NZH
                        out.append((src, dst * NX + x2 % NX))
    return out


def shift_x(k):
    return pairs(lambda y, zl, c, zh, x: (y, zl, c, zh, x + k))


def shift_y(k):
    return pairs(lambda y, zl, c, zh, x: (y + k, zl, c, zh, x))


def shift_z(k):
    def move(y, zl, c, zh, x):
        z = (zh * NZL + zl + k) % (NZH * NZL)
        return y, z % NZL, c, z // NZL, x

    return pairs(move)


def shift_zl(k):
    return pairs(lambda y, zl, c, zh, x: (y, zl + k, c, zh, x))


SWAP_CORE = pairs(lambda y, zl, c, zh, x: (y, zl, c + 1, zh, x))
RIGHT, LEFT = shift_x(1), shift_x(-1)
ACROSS = shift_z(4)


def send(value, plan):
    return lax.ppermute(value, AXES, plan)


def pick(array, index, axis=0):
    return lax.dynamic_index_in_dim(array, index, axis, keepdims=False)


def dot(left, right):
    return jnp.dot(left, right, preferred_element_type=f32)


def row_contract(left, right):
    return lax.dot_general(left, right, (((0,), (0,)), ((), ())), preferred_element_type=f32)


def by_place(pieces, place):
    count = len(pieces)
    out = jnp.zeros((count,) + pieces[0].shape, pieces[0].dtype)
    for s, piece in enumerate(pieces):
        out = lax.dynamic_update_index_in_dim(out, piece, (place - s) % count, 0)
    return out


def energy_score(samples, goal_rows):
    n_draws = samples.shape[1]
    diff_t = samples - goal_rows[:, None, :]
    dist_t = jnp.sqrt(jnp.sum(diff_t * diff_t, axis=-1) + 1.0)
    diff_p = samples[:, :, None, :] - samples[:, None, :, :]
    dist_p = jnp.sqrt(jnp.sum(diff_p * diff_p, axis=-1) + 1.0)
    off_diag = 1.0 - jnp.eye(n_draws, dtype=f32)
    pair_count = n_draws * (n_draws - 1)
    energies = jnp.mean(dist_t, axis=1) - jnp.sum(dist_p * off_diag, axis=(1, 2)) / (
        2.0 * pair_count
    )
    slopes = (
        diff_t / (n_draws * dist_t[..., None])
        - jnp.sum(diff_p / dist_p[..., None], axis=2) / pair_count
    )
    return energies, slopes.astype(bf16)


def silu_slope(values):
    sigmoid = jax.nn.sigmoid(values)
    return sigmoid * (1.0 + values * (1.0 - sigmoid))


def after(value, *first):
    return lax.optimization_barrier((value,) + first)[0]


def project(att, out_proj, residual, norm_gain, zh, x, n):
    m = att.shape[3]
    half = D // 2

    def rows(step, r):
        block = pick(att[:, :, r], (x + step) % NX, 1)
        return jnp.concatenate([pick(block, zh), pick(block, 1 - zh)], axis=0)

    w0, w1 = out_proj[:, :half], out_proj[:, half:]
    far, plain = [], []
    for r in range(n):
        lhs = rows(2, r)
        if far:
            lhs = after(lhs, *far[-1])
        far.append((dot(lhs, w0).astype(bf16), dot(lhs, w1).astype(bf16)))
    for r in range(n):
        plain.append(
            (
                dot(after(rows(1, r), *far[-1]), w1).astype(bf16),
                dot(after(rows(3, r), *far[-1]), w0).astype(bf16),
            )
        )
    marks, normed = [far[0][1], plain[1][1]], []
    far = [(send(a, RIGHT), send(b, LEFT)) for a, b in far]
    first, waiting = plain[0], []
    for r in range(n):
        right = (dot(after(rows(1, r), *first), w0) + far[r][0].astype(f32)).astype(bf16)
        left = (dot(after(rows(3, r), *first), w1) + far[r][1].astype(f32)).astype(bf16)
        right = jnp.concatenate([right, plain[r][0]], axis=1)
        left = jnp.concatenate([plain[r][1], left], axis=1)
        first = (left,)
        marks.append(left)
        from_left = send(right, RIGHT)
        from_right = send(left, LEFT)
        total = dot(rows(0, r), out_proj) + from_left.astype(f32) + from_right.astype(f32)
        out = total[m:].astype(bf16)
        if normed:
            out = after(out, normed[-1])
        waiting.append((residual[r * m : r * m + m].astype(f32) + total[:m], send(out, ACROSS)))
        if not normed:
            normed.append(finish_rows(*waiting[0], norm_gain))
    return normed + waiting[1:], marks


def finish_rows(base, crossed, norm_gain):
    h = base + crossed.astype(f32)
    scale = lax.rsqrt(jnp.mean(h * h, axis=-1, keepdims=True) + 1e-05)
    return (h * scale * norm_gain).astype(bf16)


def other_weights(cond_proj, noise_proj, latent_proj, y, core, marks):
    width = cond_proj.shape[1]
    rows = cond_proj.shape[0] // (NY * NC)
    share = lax.dynamic_slice_in_dim(cond_proj, (y * NC + core) * rows, rows, 0)
    latent = jnp.concatenate([latent_proj[:LAT], latent_proj[LAT:]], axis=1)
    packed = jnp.concatenate([share, noise_proj, latent], axis=0)
    packed = after(send(after(packed, marks[0]), ACROSS), marks[1])
    mine, noise, latent = packed[:rows], packed[rows : rows + NZ], packed[rows + NZ :]
    pieces = [mine, send(mine, shift_y(1)), send(mine, shift_y(2)), send(mine, shift_y(3))]
    held = by_place(pieces, y)
    other = send(after(held, marks[2]), SWAP_CORE)
    first = jnp.where(core == 0, held, other)
    second = jnp.where(core == 0, other, held)
    return (
        jnp.stack([first, second], axis=1).reshape(cond_proj.shape),
        noise,
        jnp.concatenate([latent[:, :LAT], latent[:, LAT:]], axis=0),
    )


def gather_rows(own):
    half = D // 2
    left, right = send(own, RIGHT), send(own, LEFT)
    far = (send(left[:, :half], RIGHT), send(right[:, half:], LEFT))
    return [
        jnp.concatenate([part[:, i * half : i * half + half] for part in (own, left, right)] + [far[i]])
        for i in range(2)
    ]


def reduce_samples(partial):
    own, left, right, far = partial
    others = (
        send(far.astype(bf16), shift_x(2)),
        send(right.astype(bf16), RIGHT),
        send(left.astype(bf16), LEFT),
    )
    return own + sum(o.astype(f32) for o in others)


def gather_slopes(own):
    return jnp.concatenate(
        [own, send(own, RIGHT), send(own, LEFT), send(own, shift_x(2))], axis=0
    )


def butterfly(value, *plans):
    for plan in plans:
        value = value + send(value, plan)
    return value


def on_device(
    attended,
    out_proj,
    residual,
    norm_gain,
    cond_proj,
    noise_proj,
    latent_proj,
    noise_draws,
    targets,
):
    y, zl = lax.axis_index("y"), lax.axis_index("zl")
    core, zh, x = lax.axis_index("core"), lax.axis_index("zh"), lax.axis_index("x")
    n = CHUNKS
    m = residual.shape[0] // n
    width = cond_proj.shape[1]
    att = attended.reshape(NZH, NX, n, m, attended.shape[1])
    noise = pick(noise_draws.reshape(NZH, NX, n, m * S, NZ), zh)
    goals = targets.astype(f32)

    def both(block, other, axis):
        return jnp.concatenate(
            [jnp.where(zh == 0, block, other), jnp.where(zh == 0, other, block)], axis=axis
        )

    normed, marks = project(att, out_proj, residual, norm_gain, zh, x, n)
    other = other_weights(cond_proj, noise_proj, latent_proj, y, core, marks)
    cond_w = both(cond_proj, other[0], 1)
    noise_w = both(noise_proj, other[1], 1)
    latent_w = both(latent_proj, other[2], 0)

    grads = []
    energies = []
    for r in range(n):
        if r:
            normed[r] = finish_rows(normed[r][0], after(normed[r][1], partial), norm_gain)
        rows = gather_rows(normed[r])
        condition = dot(rows[0], cond_w[: D // 2]) + dot(rows[1], cond_w[D // 2 :])
        draws = jnp.concatenate(
            [pick(noise, (x + step) % NX)[r] for step in (0, 3, 1, 2)], axis=0
        )
        preact = condition[:, None, :] + dot(draws, noise_w).reshape(NX * m, S, 2 * width)
        activation = jax.nn.silu(preact).astype(bf16).reshape(NX * m * S, 2 * width)
        if r:
            activation = after(activation, own_slopes)
        partial = dot(activation, latent_w).reshape(NX, m * S, LAT)
        own = reduce_samples([partial[i] for i in range(NX)])
        if r:
            own = after(own, pre_grad)
        energy, own_slopes = energy_score(own.reshape(m, S, LAT), goals[r * m : r * m + m])
        energies.append(energy)
        slopes = gather_slopes(own_slopes.reshape(m * S, LAT))
        if grads:
            slopes = after(slopes, *grads[-1])
        backward = lax.dot_general(
            slopes, latent_w, (((1,), (1,)), ((), ())), preferred_element_type=f32
        ).reshape(preact.shape)
        pre_grad = (backward * silu_slope(preact)).astype(bf16)
        cond_slope = jnp.sum(pre_grad, axis=1, dtype=f32).astype(bf16)
        grads.append(
            (
                row_contract(draws, pre_grad.reshape(activation.shape)),
                row_contract(slopes, activation),
            )
            + tuple(
                row_contract(
                    jnp.where(second, rows[1], rows[0]),
                    cond_slope[:, b * width : b * width + width],
                )
                for second in (core == 0, core == 1)
                for b in range(NZH)
            )
        )

    sums = [sum(parts) for parts in zip(*grads)]

    def share(second, cond_parts):
        blocks = []
        for b, cond_part in enumerate(cond_parts):
            small = jnp.where(second, sums[1], sums[0])[:, b * width : b * width + width]
            blocks.append(
                jnp.concatenate(
                    [
                        cond_part.reshape(NY, NZL, -1, width),
                        small.reshape(NY, NZL, -1, width),
                    ],
                    axis=2,
                )
            )
        return jnp.stack(blocks, axis=1)

    other_core = send(share(core == 0, sums[2:4]).astype(bf16), SWAP_CORE)
    held = share(core == 1, sums[4:6]) + other_core.astype(f32)

    total = pick(held, y)
    for step in (1, 2, 3):
        total = total + send(pick(held, (y + step) % NY).astype(bf16), shift_y(step)).astype(f32)
    place = zh * NZL + zl
    piece = pick(pick(total, zh), zl)
    for step in range(1, NZH * NZL):
        to = (place + step) % (NZH * NZL)
        part = pick(pick(total, to // NZL), to % NZL)
        piece = piece + send(part.astype(bf16), shift_z(step)).astype(f32)

    piece = piece.astype(bf16)
    quarter = by_place([piece] + [send(piece, shift_zl(s)) for s in (1, 2, 3)], zl)
    sent = [send(quarter, shift_y(s)) for s in (1, 2, 3)]
    squares = jnp.square(quarter.astype(f32)).reshape(-1, 8, 2, 128)
    squares = butterfly(
        jnp.sum(squares, axis=(0, 2)),
        ACROSS,
        pairs(lambda y, zl, c, zh, x: (y, zl, c, zh, x ^ 1)),
        pairs(lambda y, zl, c, zh, x: (y, zl, c, zh, x ^ 2)),
        pairs(lambda y, zl, c, zh, x: (y ^ 1, zl, c, zh, x)),
    )
    *sent, squares = lax.optimization_barrier((*sent, squares))
    half = by_place([quarter] + sent, y)
    other_half = send(half, SWAP_CORE)
    squares = butterfly(
        squares, pairs(lambda y, zl, c, zh, x: (y ^ 2, zl, c, zh, x)), SWAP_CORE
    )
    rescale = lax.rsqrt(jnp.sum(squares) / (D * HW + NZ * HW + HW * LAT) + 1e-06)
    other_half, rescale = lax.optimization_barrier((other_half, rescale))
    first = jnp.where(core == 0, half, other_half)
    second = jnp.where(core == 0, other_half, half)
    rows = D // (NC * NY * NZL)

    def scaled(value):
        return (value.astype(f32) * rescale).astype(bf16)

    cond_out = scaled(
        jnp.stack([first[:, :, :rows], second[:, :, :rows]], axis=0).reshape(D, width)
    )
    noise_out = scaled(first[:, :, rows:].reshape(NZ, width))
    latent_out = scaled(second[:, :, rows:].reshape(LAT, width).T)
    return (jnp.concatenate(energies), cond_out, noise_out, latent_out)


def solution(mesh):
    fine = Mesh(mesh.devices.reshape(NY, NZL, NC, NZH, NX), AXES)
    ctx, tp = ("y", "zl", "core"), ("zh", "x")
    return jax.shard_map(
        on_device,
        mesh=fine,
        in_specs=(
            P(ctx, tp),
            P(tp, None),
            P(AXES, None),
            P(),
            P(None, tp),
            P(None, tp),
            P(tp, None),
            P(ctx, None, None),
            P(AXES, None),
        ),
        out_specs=(P(AXES), P(None, tp), P(None, tp), P(tp, None)),
        check_vma=False,
    )
```
